768 devices in a mesh: row: 48 (over z, y_lo, core), col: 16 (over x, y_hi).
Axes of the slice: x: 4, y: 8 (y_hi: 4, y_lo: 2; y = y_hi * 2 + y_lo), z: 12, core: 2. Of those that a mesh axis runs over, the one named last changes fastest.
Arguments:
- blocks: float32 [144, 16, 4096], P('row', 'col'), may hold values from -0.75 to 0.75
- block_cols: int32 [144, 16], replicated, may hold values from 0 to 8, as said below
- product_cols: int32 [144, 16, 4], replicated, may hold values from 0 to 8, as said below
- group_sizes: int32 [144], replicated, may hold values from 32 to 64, as said below
Outputs:
- purified: float32 [144, 16, 4, 4096], P('row', 'col')
The draws below stay inside these ranges and needn't reach their ends.
Inputs may be any that keep to these rules, and one draw needn't show every extreme that they name: Block row i holds exactly one stored block in each column segment c, at column c * 9 + block_cols[i, c]. Kept product block (i, c, q) lies at column c * 9 + product_cols[i, c, q]; each is reached by at least one path i to k to j through stored blocks; a column may be kept twice in a segment. `group_sizes`: rows and columns of a block at or past its group size are padding.
All inputs are finite; a program needn't handle non-finite values.
Results may differ from the reference program's by a relative error of at most 0.0003.
Values sent between devices are 32-bit elements; how exact they have to be, the bound alone decides.
A program may use at most 64 MiB of HBM per device.

```python
import jax
import jax.numpy as jnp
from jax import lax

BS = 64
BSQ = 4096
QS = 4
NB = 144
N_COL = 16


def pattern_draw(key):
    return jax.random.randint(key, (NB, N_COL), 0, NB // N_COL, dtype=jnp.int32)


def draw_block_cols(key, part):
    shared = pattern_draw(key)
    return shared


def draw_product_cols(key, part):
    shared = pattern_draw(key)
    key = jax.random.fold_in(key, 11)
    seg_len = NB // N_COL
    via_segment = jax.random.randint(key, (NB, N_COL, QS), 0, N_COL, dtype=jnp.int32)
    row_ids = jnp.arange(NB, dtype=jnp.int32)[:, None, None]
    middle = via_segment * seg_len + shared[row_ids, via_segment]
    col_ids = jnp.arange(N_COL, dtype=jnp.int32)[None, :, None]
    return shared[middle, col_ids].astype(jnp.int32)


def draw_group_sizes(key, part):
    key = jax.random.fold_in(key, 5)
    first_key, second_key = jax.random.split(key)
    sizes = jax.random.randint(first_key, (NB,), BS // 2, BS + 1, dtype=jnp.int32)
    fullest = jax.random.randint(second_key, (), 0, NB, dtype=jnp.int32)
    return jnp.where(jnp.arange(NB, dtype=jnp.int32) == fullest, BS, sizes).astype(jnp.int32)


def levels(own_key, extent, cuts, least, largest):
    gain = 1.0
    for dim, parts in cuts:
        heights = jax.random.uniform(jax.random.fold_in(jax.random.fold_in(own_key, 6), dim), (parts,), jnp.float32, least / len(cuts), largest / len(cuts))
        gain = gain * jnp.repeat(jnp.exp(heights), extent[dim] // parts).reshape((-1,) + (1,) * (len(extent) - 1 - dim))
    return gain


def noise(stream_key, dims, deviation, reach, shards=(), kind=jnp.bfloat16):
    array = deviation * jax.random.normal(stream_key, dims, jnp.float32)
    if shards:
        array = array * levels(stream_key, dims, shards, -0.22, 0.18)
    return jnp.clip(array, -reach, reach).astype(kind)


def setup_inputs(seed: int = 0) -> dict:
    seeds = jax.random.split(jax.random.key(seed), 5)
    blocks = noise(seeds[0], (NB, N_COL, BSQ), (1.0 / BS ** 0.5), 0.75, ((0, 48), (1, 16)), jnp.float32)
    block_cols = draw_block_cols(jax.random.fold_in(seeds[4], 71), 0)
    product_cols = draw_product_cols(jax.random.fold_in(seeds[4], 71), 0)
    group_sizes = draw_group_sizes(jax.random.fold_in(seeds[4], 71), 0)
    return {"blocks": blocks, "block_cols": block_cols, "product_cols": product_cols, "group_sizes": group_sizes}


def block_mask(group_sizes, row_ids, col_ids):
    positions = jnp.arange(BS, dtype=jnp.int32)
    row_live = (positions < group_sizes[row_ids][..., None]).astype(jnp.float32)
    col_live = (positions < group_sizes[col_ids][..., None]).astype(jnp.float32)
    return row_live[..., :, None] * col_live[..., None, :]


def reference(blocks, block_cols, product_cols, group_sizes):
    seg_len = NB // N_COL
    segments = jnp.arange(N_COL, dtype=jnp.int32)
    global_cols = segments[None, :] * seg_len + block_cols
    row_ids = jnp.broadcast_to(jnp.arange(NB, dtype=jnp.int32)[:, None], (NB, N_COL))
    masked = blocks.reshape(NB, N_COL, BS, BS) * block_mask(group_sizes, row_ids, global_cols)
    highest = lax.Precision.HIGHEST

    def one_row(row_index):
        left_blocks = masked[row_index]
        inner_rows = global_cols[row_index]
        right_blocks = masked[inner_rows]
        products = jnp.einsum("sab,scbd->scad", left_blocks, right_blocks, precision=highest)
        target = product_cols[row_index]
        arrive = block_cols[inner_rows]
        matches = (arrive[:, :, None] == target[None]).astype(jnp.float32)
        square_part = jnp.einsum("scq,scad->cqad", matches, products, precision=highest)
        inner_two = segments[:, None] * seg_len + target
        right_two = masked[inner_two]
        products_two = jnp.einsum("puab,pucbd->pucad", square_part, right_two, precision=highest)
        arrive_two = block_cols[inner_two]
        matches_two = (arrive_two[..., None] == target[None, None]).astype(jnp.float32)
        cube_part = jnp.einsum("pucq,pucad->cqad", matches_two, products_two, precision=highest)
        return (3.0 * square_part - 2.0 * cube_part).reshape(N_COL, QS, BSQ)

    return lax.map(one_row, jnp.arange(NB, dtype=jnp.int32))
```

```python
import functools

import jax
import jax.numpy as jnp
from jax import lax
from jax.experimental import pallas as pl
from jax.experimental.pallas import tpu as pltpu
from jax.sharding import PartitionSpec as P

RB = 3
NZ = 12
N_COL = 16
SEG = 9
NB = 144
QS = 4
F32 = jnp.float32
BF16 = jnp.bfloat16
MESH = pl.DeviceIdType.MESH

PLUS_PARTS = {0: (0,), 1: (0, 1), 2: (0,), 3: (0, 1)}


def split(v):
    hi = v.astype(BF16)
    return hi, (v - hi.astype(F32)).astype(BF16)


def kernel(
    own_ref, bct_ref, pct_ref, size_ref, out_ref,
    strip, rows, squares, dup_hi, dup_lo, cube, wide,
    send_sem, z_sem, y_sem, sib_sem, row_sem, sq_sem,
):
    r = lax.axis_index("row")
    c = lax.axis_index("col")
    z, l, o = r // 4, (r // 2) % 2, r % 2
    x, h = c // 4, c % 4

    def dev(dz=0, flip_l=False, flip_o=False, dx=0, dh=0):
        zz = lax.rem(z + dz + NZ, NZ)
        ll = 1 - l if flip_l else l
        oo = 1 - o if flip_o else o
        xx = lax.rem(x + dx + 4, 4)
        hh = lax.rem(h + dh + 4, 4)
        return ((zz * 2 + ll) * 2 + oo, xx * 4 + hh)

    neighbours = [
        dev(dz=1), dev(dz=-1), dev(flip_l=True), dev(flip_o=True),
        dev(dx=1), dev(dx=-1), dev(dh=1), dev(dh=-1),
    ]
    barrier = pltpu.get_barrier_semaphore()
    for other in neighbours:
        pl.semaphore_signal(barrier, inc=1, device_id=other, device_id_type=MESH)

    lane = lax.broadcasted_iota(jnp.int32, (32, 128), 1)
    left = lane < 64
    in_row = lax.broadcasted_iota(jnp.int32, (32, 128), 0) + jnp.where(left, 0, 32)
    in_col = lax.rem(lane, 64)

    def turn(v):
        return pltpu.roll(v, 64, 1)

    for b in range(RB):
        t = own_ref[b]
        wide[pl.ds(0, 32, stride=2), :] = t
        wide[pl.ds(1, 32, stride=2), :] = turn(t)
        packed = jnp.where(left, wide[0:32, :], turn(wide[32:64, :]))
        row_size = size_ref[r * RB + b]
        col_size = size_ref[c * SEG + bct_ref[c, r * RB + b]]
        packed = jnp.where((in_row < row_size) & (in_col < col_size), packed, 0.0)
        strip[r * RB + b] = packed
        rows[c, b] = packed

    pl.semaphore_wait(barrier, len(neighbours))

    started = []

    def push(ref, sem, target):
        copy = pltpu.make_async_remote_copy(
            src_ref=ref, dst_ref=ref, send_sem=send_sem.at[len(started)], recv_sem=sem,
            device_id=target, device_id_type=MESH,
        )
        copy.start()
        started.append(copy)

    def arrived(ref, sem):
        pltpu.make_async_remote_copy(
            src_ref=ref, dst_ref=ref, send_sem=send_sem.at[0], recv_sem=sem,
            device_id=neighbours[0], device_id_type=MESH,
        ).wait_recv()

    class Plane:
        def __init__(self, buf, sem, parts):
            self.buf, self.sem, self.parts = buf, sem, parts

        def at(self, dx, dh, part):
            slot = lax.rem(x + dx, 4) * 4 + lax.rem(h + dh, 4)
            lo, n = self.parts[part]
            return self.buf.at[slot, pl.ds(lo, n)]

        def wait(self, dx, dh, part):
            arrived(self.at(dx, dh, part), self.sem.at[(dx * 4 + dh) * 3 + part])

        def send(self, dx, dh, part, ax, step):
            to_dx = (dx - step) % 4 if ax == "x" else dx
            to_dh = (dh - step) % 4 if ax == "h" else dh
            target = dev(dx=step) if ax == "x" else dev(dh=step)
            push(self.at(dx, dh, part), self.sem.at[(to_dx * 4 + to_dh) * 3 + part], target)

        def own(self, part):
            for ax in ("x", "h"):
                for step in (1, -1):
                    self.send(0, 0, part, ax, step)

        def near_h(self, dh, then=None):
            step = 1 if dh == 3 else -1
            for part in range(len(self.parts)):
                self.wait(0, dh, part)
                if (part in PLUS_PARTS[0]) == (step == 1):
                    self.send(0, dh, part, "h", step)
                for side in (1, -1):
                    self.send(0, dh, part, "x", side)
                if then:
                    then(0, dh, part)

        def far_h(self, then=None):
            for part in range(len(self.parts)):
                self.wait(0, 2, part)
                for side in (1, -1):
                    self.send(0, 2, part, "x", side)
                if then:
                    then(0, 2, part)

        def near_x(self, dh, then=None):
            for part in range(len(self.parts)):
                for dx in (3, 1):
                    step = 1 if dx == 3 else -1
                    self.wait(dx, dh, part)
                    if (part in PLUS_PARTS[dh]) == (step == 1):
                        self.send(dx, dh, part, "x", step)
                if then:
                    for dx in (3, 1):
                        then(dx, dh, part)

        def far_x(self, dh, then=None):
            for part in range(len(self.parts)):
                self.wait(2, dh, part)
                if then:
                    then(2, dh, part)

    row_plane = Plane(rows, row_sem, ((0, 1), (1, 1), (2, 1)))
    sq_plane = Plane(squares, sq_sem, ((0, 1), (1, 1), (2, 1)))

    def tile(dz, flip_l, flip_o, lo=0, n=RB):
        zz = lax.rem(z + dz + NZ, NZ)
        ll = 1 - l if flip_l else l
        oo = 1 - o if flip_o else o
        return strip.at[pl.ds(((zz * 2 + ll) * 2 + oo) * RB + lo, n)]

    UNITS = ((False, 0, 1), (False, 1, 2), (True, 0, 1))
    LAST = {1: (1,), -1: (0, 2)}
    half = NZ // 2

    def unit(dz, k):
        flip, lo, n = UNITS[k]
        return tile(dz, flip, False, lo, n)

    def zsem(step, t, k):
        return z_sem.at[((0 if step == 1 else 1) * (half + 1) + t) * 3 + k]

    def ysem(dz):
        return y_sem.at[dz + half]

    def sibsem(dz, flip):
        return sib_sem.at[(dz + half) * 2 + int(flip)]

    def unpack(dz, flip_l, flip_o):
        zz = lax.rem(z + dz + NZ, NZ)
        ll = 1 - l if flip_l else l
        oo = 1 - o if flip_o else o
        first = ((zz * 2 + ll) * 2 + oo) * RB

        def one(b, carry):
            t = strip[first + b]
            s = turn(t)
            for part, v in enumerate((jnp.where(left, t, s), jnp.where(left, s, t))):
                hi, lo = split(v)
                dup_hi[first + b, 2 * part : 2 * part + 2] = hi.reshape(2, 16, 128)
                dup_lo[first + b, 2 * part : 2 * part + 2] = lo.reshape(2, 16, 128)
            return carry

        lax.fori_loop(0, RB, one, 0)

    for k in (0, 1):
        for step in (1, -1):
            push(unit(0, k), zsem(step, 1, k), dev(dz=step))
        if k == 0:
            push(tile(0, False, False, 0, 1), y_sem.at[2 * half + 1], dev(flip_l=True))
    push(tile(0, False, False, 1, 2), ysem(0), dev(flip_l=True))
    for part in range(3):
        row_plane.own(part)
    push(tile(0, False, False), sibsem(0, False), dev(flip_o=True))
    unpack(0, False, False)
    arrived(tile(0, True, False, 0, 1), y_sem.at[2 * half + 1])
    for step in (1, -1):
        push(unit(0, 2), zsem(step, 1, 2), dev(dz=step))

    def other_plane(dz):
        arrived(tile(dz, True, False, 1, 2), ysem(dz))
        push(tile(dz, True, False), sibsem(dz, True), dev(flip_o=True))

    def from_sibling(dz, flip):
        arrived(tile(dz, flip, True), sibsem(dz, flip))
        unpack(dz, flip, True)

    col_events = {
        1: [lambda: row_plane.near_h(3), lambda: row_plane.near_h(1)],
        2: [lambda: row_plane.near_x(0), lambda: row_plane.far_h()],
        3: [lambda: row_plane.near_x(3), lambda: row_plane.near_x(1)],
        4: [lambda: row_plane.near_x(2)],
    }
    for t in range(1, half):
        for k in range(3):
            for step in (1, -1):
                dz = -t * step
                arrived(unit(dz, k), zsem(step, t, k))
                if t + 1 < half or k in LAST[step]:
                    push(unit(dz, k), zsem(step, t + 1, k), dev(dz=step))
                if k == 1:
                    push(tile(dz, False, False, 1, 2), ysem(dz), dev(flip_l=True))
                    push(tile(dz, False, False), sibsem(dz, False), dev(flip_o=True))
        before = [0] if t == 1 else [t - 1, 1 - t]
        for dz in before:
            other_plane(dz)
        for event in col_events.get(t, ()):
            event()
        for dz in (t, -t):
            unpack(dz, False, False)
        for dz in before:
            unpack(dz, True, False)
            from_sibling(dz, False)
        if t >= 2:
            for dz in [0] if t == 2 else [t - 2, 2 - t]:
                from_sibling(dz, True)

    dz = half
    arrived(unit(dz, 1), zsem(1, half, 1))
    push(tile(dz, False, False, 1, 2), ysem(dz), dev(flip_l=True))
    arrived(unit(dz, 0), zsem(-1, half, 0))
    push(tile(dz, False, False), sibsem(dz, False), dev(flip_o=True))
    arrived(unit(dz, 2), zsem(-1, half, 2))
    for d in (half - 1, 1 - half, half):
        other_plane(d)
    for dh in range(4):
        row_plane.far_x(dh)
    unpack(half, False, False)
    for d in (half - 2, 2 - half):
        from_sibling(d, True)
    for d in (half - 1, 1 - half, half):
        unpack(d, True, False)
        from_sibling(d, False)
    for d in (half - 1, 1 - half, half):
        from_sibling(d, True)

    q_of = lax.broadcasted_iota(jnp.int32, (16, 256), 1) // 64

    def targets(row):
        v = jnp.zeros((16, 256), jnp.int32)
        for q in range(QS):
            v = jnp.where(q_of == q, pct_ref[c, q, row], v)
        return v

    def right(inner, target):
        his, los = [], []
        for k in inner:
            m = jnp.where(target == bct_ref[c, k], 1.0, 0.0).astype(BF16)
            for ref, got in ((dup_hi, his), (dup_lo, los)):
                v = ref[k]
                v = jnp.concatenate([v, v], axis=2) * m[None]
                got.append(v.reshape(64, 256))
        return jnp.concatenate(his, axis=0), jnp.concatenate(los, axis=0)

    def product(lhs, inner, target):
        r_hi, r_lo = right(inner, target)
        l_hi, l_lo = split(lhs)
        both = jnp.dot(jnp.concatenate([l_hi, l_lo], axis=0), r_hi, preferred_element_type=F32)
        return both[:64] + both[64:] + jnp.dot(l_hi, r_lo, preferred_element_type=F32)

    for i in range(RB):
        row = r * RB + i
        target = targets(row)

        def square_step(g, acc):
            t = [rows[g * 4 + s, i] for s in range(4)]
            s = [turn(v) for v in t]
            top = [jnp.where(left, t[0], s[1]), jnp.where(left, t[2], s[3])]
            low = [jnp.where(left, s[0], t[1]), jnp.where(left, s[2], t[3])]
            lhs = jnp.concatenate(
                [jnp.concatenate(top, axis=1), jnp.concatenate(low, axis=1)], axis=0
            )
            inner = [(g * 4 + s) * SEG + bct_ref[g * 4 + s, row] for s in range(4)]
            return acc + product(lhs, inner, target)

        squares[c, i] = lax.fori_loop(0, 4, square_step, jnp.zeros((64, 256), F32))
        sq_plane.own(i)

    def cube_step(dx, dh, i, first=False):
        p = lax.rem(x + dx, 4) * 4 + lax.rem(h + dh, 4)
        row = r * RB + i
        inner = [p * SEG + pct_ref[p, u, row] for u in range(QS)]
        v = product(squares[p, i], inner, targets(row))
        cube[i] = v if first else cube[i] + v

    for i in range(RB):
        cube_step(0, 0, i, True)
    sq_plane.near_h(3)
    sq_plane.near_h(1)

    def cubes(*tiles):
        for dx, dh in tiles:
            lax.fori_loop(0, RB, lambda i, k: (cube_step(dx, dh, i), k)[1], 0)

    cubes((0, 3))
    sq_plane.near_x(0)
    cubes((0, 1))
    sq_plane.far_h()
    cubes((3, 0), (1, 0))
    sq_plane.near_x(3)
    cubes((0, 2), (3, 3))
    sq_plane.near_x(1)
    cubes((1, 3), (3, 1))
    sq_plane.far_x(0)
    sq_plane.near_x(2)
    cubes((1, 1), (2, 0))
    sq_plane.far_x(3)
    cubes((3, 2), (1, 2), (2, 3))
    sq_plane.far_x(1)
    cubes((2, 1))
    sq_plane.far_x(2)
    cubes((2, 2))

    for i in range(RB):
        wide2 = 3.0 * squares[c, i] - 2.0 * cube[i]
        for side in range(2):
            wide[:, :] = wide2[:, 128 * side : 128 * side + 128]
            even = wide[pl.ds(0, 32, stride=2), :]
            odd = wide[pl.ds(1, 32, stride=2), :]
            out_ref[i, :, 2 * side, :] = jnp.where(left, even, turn(odd))
            out_ref[i, :, 2 * side + 1, :] = jnp.where(left, turn(even), odd)

    for copy in started:
        copy.wait_send()


def per_device(blocks, block_cols, product_cols, group_sizes):
    vmem = pl.BlockSpec(memory_space=pltpu.VMEM)
    smem = pl.BlockSpec(memory_space=pltpu.SMEM)
    out = pl.pallas_call(
        kernel,
        out_shape=jax.ShapeDtypeStruct((RB, 32, QS, 128), F32),
        in_specs=[vmem, smem, smem, smem],
        out_specs=vmem,
        scratch_shapes=[
            pltpu.VMEM((NB, 32, 128), F32),
            pltpu.VMEM((N_COL, RB, 32, 128), F32),
            pltpu.VMEM((N_COL, RB, 64, 256), F32),
            pltpu.VMEM((NB, 4, 16, 128), BF16),
            pltpu.VMEM((NB, 4, 16, 128), BF16),
            pltpu.VMEM((RB, 64, 256), F32),
            pltpu.VMEM((64, 128), F32),
            pltpu.SemaphoreType.DMA((180,)),
            pltpu.SemaphoreType.DMA((42,)),
            pltpu.SemaphoreType.DMA((14,)),
            pltpu.SemaphoreType.DMA((26,)),
            pltpu.SemaphoreType.DMA((48,)),
            pltpu.SemaphoreType.DMA((48,)),
        ],
        compiler_params=pltpu.CompilerParams(
            collective_id=0, has_side_effects=True, vmem_limit_bytes=32 * 1024 * 1024
        ),
    )(
        blocks.reshape(RB, 32, 128),
        block_cols.T,
        jnp.transpose(product_cols, (1, 2, 0)),
        group_sizes,
    )
    return jnp.transpose(out, (0, 2, 1, 3)).reshape(RB, 1, QS, 4096)


def solution(mesh):
    return jax.shard_map(
        per_device,
        mesh=mesh,
        in_specs=(P("row", "col", None), P(), P(), P()),
        out_specs=P("row", "col", None, None),
        check_vma=False,
    )
```

```python
import functools

import jax
import jax.numpy as jnp
from jax import lax
from jax.experimental import pallas as pl
from jax.experimental.pallas import tpu as pltpu
from jax.sharding import PartitionSpec as P

RB = 3
NZ = 12
N_COL = 16
SEG = 9
HOP = 3
NB = 144
QS = 4
F32 = jnp.float32
BF16 = jnp.bfloat16
MESH = pl.DeviceIdType.MESH

PLUS_PARTS = {0: (0,), 1: (0, 1), 2: (0,), 3: (0, 1)}


def split(v):
    hi = v.astype(BF16)
    return hi, (v - hi.astype(F32)).astype(BF16)


def kernel(
    own_hbm, bct_hbm, pct_hbm, size_hbm, out_ref,
    own_ref, bct_ref, pct_ref, size_ref, load_sem,
    strip, rows, squares, dup_hi, dup_lo, cube, wide,
    send_sem, z_sem, y_sem, sib_sem, row_sem, sq_sem,
):
    r = lax.axis_index("row")
    c = lax.axis_index("col")
    z, l, o = r // 4, (r // 2) % 2, r % 2
    x, h = c // 4, c % 4

    def dev(dz=0, flip_l=False, flip_o=False, dx=0, dh=0):
        zz = lax.rem(z + dz + NZ, NZ)
        ll = 1 - l if flip_l else l
        oo = 1 - o if flip_o else o
        xx = lax.rem(x + dx + 4, 4)
        hh = lax.rem(h + dh + 4, 4)
        return ((zz * 2 + ll) * 2 + oo, xx * 4 + hh)

    loads = [
        pltpu.make_async_copy(src, dst, load_sem.at[k])
        for k, (src, dst) in enumerate(
            ((own_hbm, own_ref), (bct_hbm, bct_ref), (size_hbm, size_ref), (pct_hbm, pct_ref))
        )
    ]
    for load in loads:
        load.start()

    neighbours = [dev(dz=step * k) for k in range(1, HOP + 1) for step in (1, -1)] + [
        dev(flip_l=True), dev(flip_o=True), dev(dx=1), dev(dx=-1), dev(dh=1), dev(dh=-1),
    ]
    barrier = pltpu.get_barrier_semaphore()
    for other in neighbours:
        pl.semaphore_signal(barrier, inc=1, device_id=other, device_id_type=MESH)

    lane = lax.broadcasted_iota(jnp.int32, (32, 128), 1)
    left = lane < 64
    in_row = lax.broadcasted_iota(jnp.int32, (32, 128), 0) + jnp.where(left, 0, 32)
    in_col = lax.rem(lane, 64)

    def turn(v):
        return pltpu.roll(v, 64, 1)

    for load in loads[:3]:
        load.wait()

    for b in range(RB):
        t = own_ref[b]
        wide[pl.ds(0, 32, stride=2), :] = t
        wide[pl.ds(1, 32, stride=2), :] = turn(t)
        packed = jnp.where(left, wide[0:32, :], turn(wide[32:64, :]))
        row_size = size_ref[r * RB + b]
        col_size = size_ref[c * SEG + bct_ref[c, r * RB + b]]
        packed = jnp.where((in_row < row_size) & (in_col < col_size), packed, 0.0)
        strip[r * RB + b] = packed
        rows[c, b] = packed

    pl.semaphore_wait(barrier, len(neighbours))

    started = []

    def push(ref, sem, target):
        copy = pltpu.make_async_remote_copy(
            src_ref=ref, dst_ref=ref, send_sem=send_sem.at[len(started)], recv_sem=sem,
            device_id=target, device_id_type=MESH,
        )
        copy.start()
        started.append(copy)

    def arrived(ref, sem):
        pltpu.make_async_remote_copy(
            src_ref=ref, dst_ref=ref, send_sem=send_sem.at[0], recv_sem=sem,
            device_id=neighbours[0], device_id_type=MESH,
        ).wait_recv()

    class Plane:
        def __init__(self, buf, sem, parts):
            self.buf, self.sem, self.parts = buf, sem, parts

        def at(self, dx, dh, part):
            slot = lax.rem(x + dx, 4) * 4 + lax.rem(h + dh, 4)
            lo, n = self.parts[part]
            return self.buf.at[slot, pl.ds(lo, n)]

        def wait(self, dx, dh, part):
            arrived(self.at(dx, dh, part), self.sem.at[(dx * 4 + dh) * 3 + part])

        def send(self, dx, dh, part, ax, step):
            to_dx = (dx - step) % 4 if ax == "x" else dx
            to_dh = (dh - step) % 4 if ax == "h" else dh
            target = dev(dx=step) if ax == "x" else dev(dh=step)
            push(self.at(dx, dh, part), self.sem.at[(to_dx * 4 + to_dh) * 3 + part], target)

        def own(self, part):
            for ax in ("x", "h"):
                for step in (1, -1):
                    self.send(0, 0, part, ax, step)

        def near_h(self, dh, then=None):
            step = 1 if dh == 3 else -1
            for part in range(len(self.parts)):
                self.wait(0, dh, part)
                if (part in PLUS_PARTS[0]) == (step == 1):
                    self.send(0, dh, part, "h", step)
                for side in (1, -1):
                    self.send(0, dh, part, "x", side)
                if then:
                    then(0, dh, part)

        def far_h(self, then=None):
            for part in range(len(self.parts)):
                self.wait(0, 2, part)
                for side in (1, -1):
                    self.send(0, 2, part, "x", side)
                if then:
                    then(0, 2, part)

        def near_x(self, dh, then=None):
            for part in range(len(self.parts)):
                for dx in (3, 1):
                    step = 1 if dx == 3 else -1
                    self.wait(dx, dh, part)
                    if (part in PLUS_PARTS[dh]) == (step == 1):
                        self.send(dx, dh, part, "x", step)
                if then:
                    for dx in (3, 1):
                        then(dx, dh, part)

        def far_x(self, dh, then=None):
            for part in range(len(self.parts)):
                self.wait(2, dh, part)
                if then:
                    then(2, dh, part)

    row_plane = Plane(rows, row_sem, ((0, 1), (1, 1), (2, 1)))
    sq_plane = Plane(squares, sq_sem, ((0, 1), (1, 1), (2, 1)))

    def tile(dz, flip_l, flip_o, lo=0, n=RB):
        zz = lax.rem(z + dz + NZ, NZ)
        ll = 1 - l if flip_l else l
        oo = 1 - o if flip_o else o
        return strip.at[pl.ds(((zz * 2 + ll) * 2 + oo) * RB + lo, n)]

    half = NZ // 2
    FAR = {1: (0, 1), -1: (1, 2)}

    def zsem(dz, part=0):
        return z_sem.at[(dz + half) if part == 0 else 2 * half + 1]

    def ysem(dz):
        return y_sem.at[dz + half]

    def sibsem(dz, flip):
        return sib_sem.at[(dz + half) * 2 + int(flip)]

    def unpack(dz, flip_l, flip_o):
        zz = lax.rem(z + dz + NZ, NZ)
        ll = 1 - l if flip_l else l
        oo = 1 - o if flip_o else o
        first = ((zz * 2 + ll) * 2 + oo) * RB
        for b in range(RB):
            t = strip[first + b]
            s = turn(t)
            for part, v in enumerate((jnp.where(left, t, s), jnp.where(left, s, t))):
                hi, lo = split(v)
                dup_hi[first + b, 2 * part : 2 * part + 2] = hi.reshape(2, 16, 128)
                dup_lo[first + b, 2 * part : 2 * part + 2] = lo.reshape(2, 16, 128)

    def across(dz):
        push(tile(dz, False, False), ysem(dz), dev(flip_l=True))
        push(tile(dz, False, False), sibsem(dz, False), dev(flip_o=True))

    def near_z(dz):
        arrived(tile(dz, False, False), zsem(dz))
        if abs(dz) == HOP:
            step = 1 if dz < 0 else -1
            lo, n = FAR[step]
            push(tile(dz, False, False, lo, n), zsem(half, int(step < 0)), dev(dz=3 * step))
            for k in (2, 1):
                push(tile(dz, False, False), zsem(dz - k * step), dev(dz=k * step))
        across(dz)

    def other_plane(dz):
        arrived(tile(dz, True, False), ysem(dz))
        push(tile(dz, True, False), sibsem(dz, True), dev(flip_o=True))
        unpack(dz, True, False)

    def from_sibling(dz, flip):
        arrived(tile(dz, flip, True), sibsem(dz, flip))
        unpack(dz, flip, True)

    for k in range(HOP, 0, -1):
        for step in (1, -1):
            push(tile(0, False, False), zsem(-k * step), dev(dz=k * step))
    across(0)
    for part in range(3):
        row_plane.own(part)
    loads[3].wait()
    unpack(0, False, False)
    other_plane(0)
    from_sibling(0, False)
    row_plane.near_h(3)
    row_plane.near_h(1)
    for dz in (3, -3, 2, -2, 1, -1):
        near_z(dz)
    row_plane.near_x(0)
    for dz in (3, -3, 2, -2, 1, -1):
        unpack(dz, False, False)
    row_plane.far_h()
    from_sibling(0, True)
    for dz in (3, -3, 2, -2, 1, -1):
        from_sibling(dz, False)
    row_plane.near_x(3)
    row_plane.near_x(1)
    for dz in (3, -3, 2, -2):
        other_plane(dz)
    for dz in (4, -4, 5, -5):
        near_z(dz)
    for step in (1, -1):
        lo, n = FAR[step]
        arrived(tile(half, False, False, lo, n), zsem(half, int(step < 0)))
    across(half)
    row_plane.near_x(2)
    for dz in (1, -1):
        other_plane(dz)
    for dz in (4, -4, 5, -5, 6):
        unpack(dz, False, False)
    for dz in (3, -3, 2, -2, 1, -1):
        from_sibling(dz, True)
    for dh in range(4):
        row_plane.far_x(dh)
    for dz in (4, -4, 5, -5, 6):
        from_sibling(dz, False)
    for dz in (4, -4, 5, -5, 6):
        other_plane(dz)
    for dz in (4, -4, 5, -5, 6):
        from_sibling(dz, True)

    q_of = lax.broadcasted_iota(jnp.int32, (16, 256), 1) // 64

    def targets(row):
        v = jnp.zeros((16, 256), jnp.int32)
        for q in range(QS):
            v = jnp.where(q_of == q, pct_ref[c, q, row], v)
        return v

    def right(inner, target):
        his, los = [], []
        for k in inner:
            m = jnp.where(target == bct_ref[c, k], 1.0, 0.0).astype(BF16)
            for ref, got in ((dup_hi, his), (dup_lo, los)):
                v = ref[k]
                v = jnp.concatenate([v, v], axis=2) * m[None]
                got.append(v.reshape(64, 256))
        return jnp.concatenate(his, axis=0), jnp.concatenate(los, axis=0)

    def product(lhs, inner, target):
        r_hi, r_lo = right(inner, target)
        l_hi, l_lo = split(lhs)
        both = jnp.dot(jnp.concatenate([l_hi, l_lo], axis=0), r_hi, preferred_element_type=F32)
        return both[:64] + both[64:] + jnp.dot(l_hi, r_lo, preferred_element_type=F32)

    wanted = [targets(r * RB + i) for i in range(RB)]

    def square_step(g, accs):
        out = []
        for i in range(RB):
            t = [rows[g * 4 + s, i] for s in range(4)]
            s = [turn(v) for v in t]
            top = [jnp.where(left, t[0], s[1]), jnp.where(left, t[2], s[3])]
            low = [jnp.where(left, s[0], t[1]), jnp.where(left, s[2], t[3])]
            lhs = jnp.concatenate(
                [jnp.concatenate(top, axis=1), jnp.concatenate(low, axis=1)], axis=0
            )
            inner = [(g * 4 + s) * SEG + bct_ref[g * 4 + s, r * RB + i] for s in range(4)]
            out.append(accs[i] + product(lhs, inner, wanted[i]))
        return tuple(out)

    accs = lax.fori_loop(0, 4, square_step, (jnp.zeros((64, 256), F32),) * RB)
    for i in range(RB):
        squares[c, i] = accs[i]
        sq_plane.own(i)

    def cubes(*tiles):
        for dx, dh in tiles:
            p = lax.rem(x + dx, 4) * 4 + lax.rem(h + dh, 4)
            for i in range(RB):
                inner = [p * SEG + pct_ref[p, u, r * RB + i] for u in range(QS)]
                v = product(squares[p, i], inner, wanted[i])
                cube[i] = v if (dx, dh) == (0, 0) else cube[i] + v

    cubes((0, 0))
    sq_plane.near_h(3)
    sq_plane.near_h(1)

    cubes((0, 3))
    sq_plane.near_x(0)
    cubes((0, 1))
    sq_plane.far_h()
    cubes((3, 0), (1, 0))
    sq_plane.near_x(3)
    cubes((0, 2), (3, 3))
    sq_plane.near_x(1)
    cubes((1, 3), (3, 1))
    sq_plane.far_x(0)
    sq_plane.near_x(2)
    cubes((1, 1), (2, 0))
    sq_plane.far_x(3)
    cubes((3, 2), (1, 2), (2, 3))
    sq_plane.far_x(1)
    cubes((2, 1))
    sq_plane.far_x(2)
    cubes((2, 2))

    for i in range(RB):
        wide2 = 3.0 * squares[c, i] - 2.0 * cube[i]
        for side in range(2):
            wide[:, :] = wide2[:, 128 * side : 128 * side + 128]
            even = wide[pl.ds(0, 32, stride=2), :]
            odd = wide[pl.ds(1, 32, stride=2), :]
            out_ref[i, :, 2 * side, :] = jnp.where(left, even, turn(odd))
            out_ref[i, :, 2 * side + 1, :] = jnp.where(left, turn(even), odd)

    for copy in started:
        copy.wait_send()


def per_device(blocks, block_cols, product_cols, group_sizes):
    vmem = pl.BlockSpec(memory_space=pltpu.VMEM)
    out = pl.pallas_call(
        kernel,
        out_shape=jax.ShapeDtypeStruct((RB, 32, QS, 128), F32),
        in_specs=[pl.BlockSpec(memory_space=pl.ANY)] * 4,
        out_specs=vmem,
        scratch_shapes=[
            pltpu.VMEM((RB, 32, 128), F32),
            pltpu.SMEM((N_COL, NB), jnp.int32),
            pltpu.SMEM((N_COL, QS, NB), jnp.int32),
            pltpu.SMEM((NB,), jnp.int32),
            pltpu.SemaphoreType.DMA((4,)),
            pltpu.VMEM((NB, 32, 128), F32),
            pltpu.VMEM((N_COL, RB, 32, 128), F32),
            pltpu.VMEM((N_COL, RB, 64, 256), F32),
            pltpu.VMEM((NB, 4, 16, 128), BF16),
            pltpu.VMEM((NB, 4, 16, 128), BF16),
            pltpu.VMEM((RB, 64, 256), F32),
            pltpu.VMEM((64, 128), F32),
            pltpu.SemaphoreType.DMA((180,)),
            pltpu.SemaphoreType.DMA((14,)),
            pltpu.SemaphoreType.DMA((13,)),
            pltpu.SemaphoreType.DMA((26,)),
            pltpu.SemaphoreType.DMA((48,)),
            pltpu.SemaphoreType.DMA((48,)),
        ],
        compiler_params=pltpu.CompilerParams(
            collective_id=0, has_side_effects=True, vmem_limit_bytes=56 * 1024 * 1024
        ),
    )(
        blocks.reshape(RB, 32, 128),
        block_cols.T,
        jnp.transpose(product_cols, (1, 2, 0)),
        group_sizes,
    )
    return jnp.transpose(out, (0, 2, 1, 3)).reshape(RB, 1, QS, 4096)


def solution(mesh):
    return jax.shard_map(
        per_device,
        mesh=mesh,
        in_specs=(P("row", "col", None), P(), P(), P()),
        out_specs=P("row", "col", None, None),
        check_vma=False,
    )
```

```python
import functools

import jax
import jax.numpy as jnp
from jax import lax
from jax.experimental import pallas as pl
from jax.experimental.pallas import tpu as pltpu
from jax.sharding import PartitionSpec as P

RB = 3
NZ = 12
N_COL = 16
SEG = 9
HOP = 3
NB = 144
QS = 4
F32 = jnp.float32
BF16 = jnp.bfloat16
MESH = pl.DeviceIdType.MESH

PLUS_PARTS = {0: (0,), 1: (1, 2), 2: (0,), 3: (1, 2)}


def split(v):
    hi = v.astype(BF16)
    return hi, (v - hi.astype(F32)).astype(BF16)


def kernel(
    own_hbm, bct_hbm, pct_hbm, size_hbm, out_ref,
    own_ref, bct_ref, pct_ref, size_ref, load_sem,
    strip, rows, squares, dup_hi, dup_lo, cube, wide,
    twin_strip, twin_hi, twin_lo, twin_cube, back_cube,
    send_sem, z_sem, y_sem, sib_sem, row_sem, sq_sem,
    twin_sem, twin_z_sem, twin_y_sem, twin_sib_sem, back_sem,
):
    r = lax.axis_index("row")
    c = lax.axis_index("col")
    z, l, o = r // 4, (r // 2) % 2, r % 2
    x, h = c // 4, c % 4

    def dev(dz=0, flip_l=False, flip_o=False, dx=0, dh=0):
        zz = lax.rem(z + dz + NZ, NZ)
        ll = 1 - l if flip_l else l
        oo = 1 - o if flip_o else o
        xx = lax.rem(x + dx + 4, 4)
        hh = lax.rem(h + dh + 4, 4)
        return ((zz * 2 + ll) * 2 + oo, xx * 4 + hh)

    loads = [
        pltpu.make_async_copy(src, dst, load_sem.at[k])
        for k, (src, dst) in enumerate(
            ((own_hbm, own_ref), (bct_hbm, bct_ref), (size_hbm, size_ref), (pct_hbm, pct_ref))
        )
    ]
    for load in loads:
        load.start()

    neighbours = [dev(dz=step * k) for k in range(1, HOP + 1) for step in (1, -1)] + [
        dev(flip_l=True), dev(flip_o=True), dev(dx=1), dev(dx=-1), dev(dh=1), dev(dh=-1),
    ]
    barrier = pltpu.get_barrier_semaphore()
    for other in neighbours:
        pl.semaphore_signal(barrier, inc=1, device_id=other, device_id_type=MESH)

    lane = lax.broadcasted_iota(jnp.int32, (32, 128), 1)
    left = lane < 64
    in_row = lax.broadcasted_iota(jnp.int32, (32, 128), 0) + jnp.where(left, 0, 32)
    in_col = lax.rem(lane, 64)

    def turn(v):
        return pltpu.roll(v, 64, 1)

    for load in loads[:3]:
        load.wait()

    for b in range(RB):
        t = own_ref[b]
        wide[pl.ds(0, 32, stride=2), :] = t
        wide[pl.ds(1, 32, stride=2), :] = turn(t)
        packed = jnp.where(left, wide[0:32, :], turn(wide[32:64, :]))
        row_size = size_ref[r * RB + b]
        col_size = size_ref[c * SEG + bct_ref[c, r * RB + b]]
        packed = jnp.where((in_row < row_size) & (in_col < col_size), packed, 0.0)
        strip[r * RB + b] = packed
        rows[c, b] = packed

    pl.semaphore_wait(barrier, len(neighbours))

    started = []

    def when(cond, body):
        if cond is None:
            body()
        else:
            pl.when(cond)(body)

    def push(ref, sem, target, dst=None, cond=None):
        k = len(started)

        def copy():
            return pltpu.make_async_remote_copy(
                src_ref=ref, dst_ref=ref if dst is None else dst, send_sem=send_sem.at[k],
                recv_sem=sem, device_id=target, device_id_type=MESH,
            )

        started.append((cond, copy))
        when(cond, lambda: copy().start())

    def arrived(ref, sem, cond=None):
        def wait():
            pltpu.make_async_remote_copy(
                src_ref=ref, dst_ref=ref, send_sem=send_sem.at[0], recv_sem=sem,
                device_id=neighbours[0], device_id_type=MESH,
            ).wait_recv()

        when(cond, wait)

    class Plane:
        def __init__(self, buf, sem, parts):
            self.buf, self.sem, self.parts = buf, sem, parts

        def at(self, dx, dh, part):
            slot = lax.rem(x + dx, 4) * 4 + lax.rem(h + dh, 4)
            lo, n = self.parts[part]
            return self.buf.at[slot, pl.ds(lo, n)]

        def wait(self, dx, dh, part):
            arrived(self.at(dx, dh, part), self.sem.at[(dx * 4 + dh) * len(self.parts) + part])

        def send(self, dx, dh, part, ax, step):
            to_dx = (dx - step) % 4 if ax == "x" else dx
            to_dh = (dh - step) % 4 if ax == "h" else dh
            target = dev(dx=step) if ax == "x" else dev(dh=step)
            sem = self.sem.at[(to_dx * 4 + to_dh) * len(self.parts) + part]
            push(self.at(dx, dh, part), sem, target)

        def both(self, dx, dh, part, ax):
            for step in (1, -1):
                self.send(dx, dh, part, ax, step)

        def own(self, part):
            self.both(0, 0, part, "h")
            self.both(0, 0, part, "x")

        def near_h(self, dh, part):
            step = 1 if dh == 3 else -1
            self.wait(0, dh, part)
            if (part in PLUS_PARTS[0]) == (step == 1):
                self.send(0, dh, part, "h", step)
            self.both(0, dh, part, "x")

        def far_h(self, part):
            self.wait(0, 2, part)
            self.both(0, 2, part, "x")

        def near_x(self, dh, part):
            for dx in (3, 1):
                step = 1 if dx == 3 else -1
                self.wait(dx, dh, part)
                if (part in PLUS_PARTS[dh]) == (step == 1):
                    self.send(dx, dh, part, "x", step)

    THREE = (0, 1, 2)
    row_plane = Plane(rows, row_sem, ((0, 1), (1, 1), (2, 1)))

    half = NZ // 2
    FAR = {1: (0, 1), -1: (1, 2)}

    class Strip:
        def __init__(self, buf, hi, lo, z_sem, y_sem, sib_sem, held):
            self.buf, self.hi, self.lo, self.held = buf, hi, lo, held
            self.z_sem, self.y_sem, self.sib_sem = z_sem, y_sem, sib_sem

        def index(self, dz, flip_l, flip_o):
            zz = lax.rem(z + dz + NZ, NZ)
            ll = 1 - l if flip_l else l
            oo = 1 - o if flip_o else o
            return (zz * 2 + ll) * 2 + oo

        def tile(self, dz, flip_l, flip_o, lo=0, n=RB):
            return self.buf.at[pl.ds(self.index(dz, flip_l, flip_o) * RB + lo, n)]

        def cond(self, dz, flip_l, flip_o):
            return self.held(self.index(dz, flip_l, flip_o)) if self.held else None

        def z_at(self, dz, part=0):
            return self.z_sem.at[(dz + half) if part == 0 else 2 * half + 1]

        def sib_at(self, dz, flip):
            return self.sib_sem.at[(dz + half) * 2 + int(flip)]

        def unpack(self, dz, flip_l, flip_o):
            def body():
                first = self.index(dz, flip_l, flip_o) * RB
                for b in range(RB):
                    t = self.buf[first + b]
                    s = turn(t)
                    for part, v in enumerate((jnp.where(left, t, s), jnp.where(left, s, t))):
                        hi, lo = split(v)
                        self.hi[first + b, 2 * part : 2 * part + 2] = hi.reshape(2, 16, 128)
                        self.lo[first + b, 2 * part : 2 * part + 2] = lo.reshape(2, 16, 128)

            when(self.cond(dz, flip_l, flip_o), body)

        def start_z(self):
            cond = self.cond(0, False, False)
            for k in range(HOP, 0, -1):
                for step in (1, -1):
                    push(self.tile(0, False, False), self.z_at(-k * step), dev(dz=k * step), cond=cond)

        def across(self, dz):
            cond, t = self.cond(dz, False, False), self.tile(dz, False, False)
            push(t, self.y_sem.at[dz + half], dev(flip_l=True), cond=cond)
            push(t, self.sib_at(dz, False), dev(flip_o=True), cond=cond)

        def near_z(self, dz):
            cond, t = self.cond(dz, False, False), self.tile(dz, False, False)
            arrived(t, self.z_at(dz), cond)
            if abs(dz) == HOP:
                step = 1 if dz < 0 else -1
                part = self.tile(dz, False, False, *FAR[step])
                push(part, self.z_at(half, int(step < 0)), dev(dz=3 * step), cond=cond)
                for k in (2, 1):
                    push(t, self.z_at(dz - k * step), dev(dz=k * step), cond=cond)
            self.across(dz)

        def opposite(self):
            for step in (1, -1):
                part = self.tile(half, False, False, *FAR[step])
                arrived(part, self.z_at(half, int(step < 0)), self.cond(half, False, False))
            self.across(half)

        def other_plane(self, dz):
            cond, t = self.cond(dz, True, False), self.tile(dz, True, False)
            arrived(t, self.y_sem.at[dz + half], cond)
            push(t, self.sib_at(dz, True), dev(flip_o=True), cond=cond)
            self.unpack(dz, True, False)

        def from_sibling(self, dz, flip):
            arrived(self.tile(dz, flip, True), self.sib_at(dz, flip), self.cond(dz, flip, True))
            self.unpack(dz, flip, True)

    NEAR = (3, -3, 2, -2, 1, -1)
    FARTHER = (4, -4, 5, -5)
    main = Strip(strip, dup_hi, dup_lo, z_sem, y_sem, sib_sem, None)

    g = h // 2
    twin = (r, x * 4 + 3 - h)
    twin_c = x * 4 + 3 - h

    def held(index):
        return lax.rem(index // 6, 2) == g

    mine = held(r)
    other = Strip(twin_strip, twin_hi, twin_lo, twin_z_sem, twin_y_sem, twin_sib_sem, held)

    main.start_z()
    main.across(0)
    for part in THREE:
        row_plane.own(part)
    own_tile = main.tile(0, False, False)
    push(own_tile, twin_sem.at[0], twin, dst=other.tile(0, False, False), cond=jnp.logical_not(mine))
    loads[3].wait()
    main.unpack(0, False, False)
    main.other_plane(0)
    main.from_sibling(0, False)
    for dh in (3, 1):
        for part in THREE:
            row_plane.near_h(dh, part)
    for dz in NEAR:
        main.near_z(dz)
    arrived(other.tile(0, False, False), twin_sem.at[0], mine)
    other.start_z()
    for part in THREE:
        row_plane.near_x(0, part)
    for dz in NEAR:
        main.unpack(dz, False, False)
    for part in THREE:
        row_plane.far_h(part)
    main.from_sibling(0, True)
    for dz in NEAR:
        main.from_sibling(dz, False)
    for dh in (3, 1):
        for part in THREE:
            row_plane.near_x(dh, part)
    for dz in (3, -3, 2, -2):
        main.other_plane(dz)
    for dz in FARTHER:
        main.near_z(dz)
    main.opposite()
    for part in THREE:
        row_plane.near_x(2, part)
    for dz in NEAR:
        other.near_z(dz)
    other.across(0)
    for dz in (1, -1):
        main.other_plane(dz)
    for dz in FARTHER + (6,):
        main.unpack(dz, False, False)
    for dz in NEAR:
        main.from_sibling(dz, True)
    for dh in range(4):
        for part in THREE:
            row_plane.wait(2, dh, part)
    for dz in FARTHER + (6,):
        main.from_sibling(dz, False)
    for dz in FARTHER + (6,):
        main.other_plane(dz)
    for dz in FARTHER:
        other.near_z(dz)
    other.opposite()
    for dz in FARTHER + (6,):
        main.from_sibling(dz, True)

    q_of = lax.broadcasted_iota(jnp.int32, (16, 256), 1) // 64

    def targets(col, row):
        v = jnp.zeros((16, 256), jnp.int32)
        for q in range(QS):
            v = jnp.where(q_of == q, pct_ref[col, q, row], v)
        return v

    def right(inner, target, col, hi_ref, lo_ref):
        his, los = [], []
        for k in inner:
            m = jnp.where(target == bct_ref[col, k], 1.0, 0.0).astype(BF16)
            for ref, got in ((hi_ref, his), (lo_ref, los)):
                v = ref[k]
                v = jnp.concatenate([v, v], axis=2) * m[None]
                got.append(v.reshape(64, 256))
        return jnp.concatenate(his, axis=0), jnp.concatenate(los, axis=0)

    def product(lhs, inner, target, col=c, hi_ref=dup_hi, lo_ref=dup_lo):
        r_hi, r_lo = right(inner, target, col, hi_ref, lo_ref)
        l_hi, l_lo = split(lhs)
        both = jnp.dot(jnp.concatenate([l_hi, l_lo], axis=0), r_hi, preferred_element_type=F32)
        return both[:64] + both[64:] + jnp.dot(l_hi, r_lo, preferred_element_type=F32)

    wanted = [targets(c, r * RB + i) for i in range(RB)]
    twin_wanted = [targets(twin_c, r * RB + i) for i in range(RB)]

    def square_step(g, accs):
        out = []
        for i in range(RB):
            t = [rows[g * 4 + s, i] for s in range(4)]
            s = [turn(v) for v in t]
            top = [jnp.where(left, t[0], s[1]), jnp.where(left, t[2], s[3])]
            low = [jnp.where(left, s[0], t[1]), jnp.where(left, s[2], t[3])]
            lhs = jnp.concatenate(
                [jnp.concatenate(top, axis=1), jnp.concatenate(low, axis=1)], axis=0
            )
            inner = [(g * 4 + s) * SEG + bct_ref[g * 4 + s, r * RB + i] for s in range(4)]
            out.append(accs[i] + product(lhs, inner, wanted[i]))
        return tuple(out)

    accs = lax.fori_loop(0, 4, square_step, (jnp.zeros((64, 256), F32),) * RB)
    mate_h = h + 1 - 2 * lax.rem(h, 2)
    mate = (r, x * 4 + mate_h)

    def slot(dx, e):
        return lax.rem(x + dx, 4) * 4 + (mate_h if e else h)

    def sq_at(dx, e, i):
        return squares.at[slot(dx, e), pl.ds(64 * i, 64)]

    def sq_sem_at(dx, e, i):
        return sq_sem.at[(dx * 2 + e) * 3 + i]

    def sq_wait(dx, e, i):
        arrived(sq_at(dx, e, i), sq_sem_at(dx, e, i))

    def sq_along_x(e, i):
        for step in (1, -1):
            push(sq_at(0, e, i), sq_sem_at(-step % 4, e, i), dev(dx=step))

    def sq_near_x(e, i):
        for dx in (3, 1):
            step = 1 if dx == 3 else -1
            sq_wait(dx, e, i)
            if (i in PLUS_PARTS[e]) == (step == 1):
                push(sq_at(dx, e, i), sq_sem_at(2, e, i), dev(dx=step))

    def cubes(i, *tiles):
        row = r * RB + i
        for dx, e in tiles:
            p = slot(dx, e)
            lhs = squares[p, pl.ds(64 * i, 64)]
            inner = [p * SEG + pct_ref[p, u, row] for u in range(QS)]
            v = product(lhs, inner, wanted[i])
            w = product(lhs, inner, twin_wanted[i], twin_c, twin_hi, twin_lo)
            first = (dx, e) == (0, 0)
            cube[i] = v if first else cube[i] + v
            twin_cube[i] = w if first else twin_cube[i] + w

    for i in range(RB):
        squares[c, pl.ds(64 * i, 64)] = accs[i]
        push(sq_at(0, 0, i), sq_sem_at(0, 1, i), mate)
        sq_along_x(0, i)
    ALL = (0,) + NEAR + FARTHER + (6,)
    for dz in ALL:
        other.unpack(dz, False, False)
    for dz in ALL[:7]:
        other.from_sibling(dz, False)
    for i in range(RB):
        sq_near_x(0, i)
        sq_wait(0, 1, i)
        sq_along_x(1, i)
    for dz in ALL:
        other.other_plane(dz)
    for dz in ALL[7:]:
        other.from_sibling(dz, False)
    for i in range(RB):
        sq_near_x(1, i)
    for dz in ALL:
        other.from_sibling(dz, True)
    for i in range(RB):
        cubes(i, (0, 0), (3, 0), (1, 0), (0, 1))
    for i in range(RB):
        sq_wait(2, 0, i)
        sq_wait(2, 1, i)
        cubes(i, (2, 0), (3, 1), (1, 1), (2, 1))
        push(twin_cube.at[i], back_sem.at[i], twin, dst=back_cube.at[i])
    for i in range(RB):
        arrived(back_cube.at[i], back_sem.at[i])

    for i in range(RB):
        wide2 = 3.0 * squares[c, pl.ds(64 * i, 64)] - 2.0 * (cube[i] + back_cube[i])
        for side in range(2):
            wide[:, :] = wide2[:, 128 * side : 128 * side + 128]
            even = wide[pl.ds(0, 32, stride=2), :]
            odd = wide[pl.ds(1, 32, stride=2), :]
            out_ref[i, :, 2 * side, :] = jnp.where(left, even, turn(odd))
            out_ref[i, :, 2 * side + 1, :] = jnp.where(left, turn(even), odd)

    for cond, copy in started:
        when(cond, lambda copy=copy: copy().wait_send())


def per_device(blocks, block_cols, product_cols, group_sizes):
    vmem = pl.BlockSpec(memory_space=pltpu.VMEM)
    out = pl.pallas_call(
        kernel,
        out_shape=jax.ShapeDtypeStruct((RB, 32, QS, 128), F32),
        in_specs=[pl.BlockSpec(memory_space=pl.ANY)] * 4,
        out_specs=vmem,
        scratch_shapes=[
            pltpu.VMEM((RB, 32, 128), F32),
            pltpu.SMEM((N_COL, NB), jnp.int32),
            pltpu.SMEM((N_COL, QS, NB), jnp.int32),
            pltpu.SMEM((NB,), jnp.int32),
            pltpu.SemaphoreType.DMA((4,)),
            pltpu.VMEM((NB, 32, 128), F32),
            pltpu.VMEM((N_COL, RB, 32, 128), F32),
            pltpu.VMEM((N_COL, RB * 64, 256), F32),
            pltpu.VMEM((NB, 4, 16, 128), BF16),
            pltpu.VMEM((NB, 4, 16, 128), BF16),
            pltpu.VMEM((RB, 64, 256), F32),
            pltpu.VMEM((64, 128), F32),
            pltpu.VMEM((NB, 32, 128), F32),
            pltpu.VMEM((NB, 4, 16, 128), BF16),
            pltpu.VMEM((NB, 4, 16, 128), BF16),
            pltpu.VMEM((RB, 64, 256), F32),
            pltpu.VMEM((RB, 64, 256), F32),
            pltpu.SemaphoreType.DMA((180,)),
            pltpu.SemaphoreType.DMA((14,)),
            pltpu.SemaphoreType.DMA((13,)),
            pltpu.SemaphoreType.DMA((26,)),
            pltpu.SemaphoreType.DMA((48,)),
            pltpu.SemaphoreType.DMA((24,)),
            pltpu.SemaphoreType.DMA((1,)),
            pltpu.SemaphoreType.DMA((14,)),
            pltpu.SemaphoreType.DMA((13,)),
            pltpu.SemaphoreType.DMA((26,)),
            pltpu.SemaphoreType.DMA((3,)),
        ],
        compiler_params=pltpu.CompilerParams(
            collective_id=0, has_side_effects=True, vmem_limit_bytes=56 * 1024 * 1024
        ),
    )(
        blocks.reshape(RB, 32, 128),
        block_cols.T,
        jnp.transpose(product_cols, (1, 2, 0)),
        group_sizes,
    )
    return jnp.transpose(out, (0, 2, 1, 3)).reshape(RB, 1, QS, 4096)


def solution(mesh):
    return jax.shard_map(
        per_device,
        mesh=mesh,
        in_specs=(P("row", "col", None), P(), P(), P()),
        out_specs=P("row", "col", None, None),
        check_vma=False,
    )
```

```python
import functools

import jax
import jax.numpy as jnp
from jax import lax
from jax.experimental import pallas as pl
from jax.experimental.pallas import tpu as pltpu
from jax.sharding import PartitionSpec as P

RB = 3
NZ = 12
N_COL = 16
SEG = 9
HOP = 3
ONWARD = {3: (3, 2, 1)}
NB = 144
QS = 4
F32 = jnp.float32
BF16 = jnp.bfloat16
MESH = pl.DeviceIdType.MESH

PLUS_PARTS = {0: (0,), 1: (1, 2), 2: (0,), 3: (1, 2)}


def split(v):
    hi = v.astype(BF16)
    return hi, (v - hi.astype(F32)).astype(BF16)


def kernel(
    own_hbm, bct_hbm, pct_hbm, size_hbm, out_ref,
    own_ref, bct_ref, pct_ref, size_ref, load_sem,
    strip, rows, squares, dup_hi, dup_lo, cube, wide,
    twin_strip, twin_hi, twin_lo, twin_cube, back_cube,
    send_sem, z_sem, y_sem, sib_sem, row_sem, sq_sem,
    twin_sem, twin_z_sem, twin_sib_sem, back_sem,
):
    r = lax.axis_index("row")
    c = lax.axis_index("col")
    z, l, o = r // 4, (r // 2) % 2, r % 2
    x, h = c // 4, c % 4

    def dev(dz=0, flip_l=False, flip_o=False, dx=0, dh=0):
        zz = lax.rem(z + dz + NZ, NZ)
        ll = 1 - l if flip_l else l
        oo = 1 - o if flip_o else o
        xx = lax.rem(x + dx + 4, 4)
        hh = lax.rem(h + dh + 4, 4)
        return ((zz * 2 + ll) * 2 + oo, xx * 4 + hh)

    loads = [
        pltpu.make_async_copy(src, dst, load_sem.at[k])
        for k, (src, dst) in enumerate(
            ((own_hbm, own_ref), (bct_hbm, bct_ref), (size_hbm, size_ref), (pct_hbm, pct_ref))
        )
    ]
    for load in loads:
        load.start()

    neighbours = [dev(dz=step * k) for k in range(1, HOP + 1) for step in (1, -1)] + [
        dev(flip_l=True), dev(flip_o=True), dev(dx=1), dev(dx=-1), dev(dh=1), dev(dh=-1),
        (dev(flip_l=True)[0], x * 4 + 3 - h),
    ]
    barrier = pltpu.get_barrier_semaphore()
    for other in neighbours:
        pl.semaphore_signal(barrier, inc=1, device_id=other, device_id_type=MESH)

    lane = lax.broadcasted_iota(jnp.int32, (32, 128), 1)
    left = lane < 64
    in_row = lax.broadcasted_iota(jnp.int32, (32, 128), 0) + jnp.where(left, 0, 32)
    in_col = lax.rem(lane, 64)

    def turn(v):
        return pltpu.roll(v, 64, 1)

    for load in loads[:3]:
        load.wait()

    for b in range(RB):
        t = own_ref[b]
        wide[pl.ds(0, 32, stride=2), :] = t
        wide[pl.ds(1, 32, stride=2), :] = turn(t)
        packed = jnp.where(left, wide[0:32, :], turn(wide[32:64, :]))
        row_size = size_ref[r * RB + b]
        col_size = size_ref[c * SEG + bct_ref[c, r * RB + b]]
        packed = jnp.where((in_row < row_size) & (in_col < col_size), packed, 0.0)
        strip[r * RB + b] = packed
        rows[c, b] = packed

    pl.semaphore_wait(barrier, len(neighbours))

    started = []

    def when(cond, body):
        if cond is None:
            body()
        else:
            pl.when(cond)(body)

    def push(ref, sem, target, dst=None, cond=None):
        k = len(started)

        def copy():
            return pltpu.make_async_remote_copy(
                src_ref=ref, dst_ref=ref if dst is None else dst, send_sem=send_sem.at[k],
                recv_sem=sem, device_id=target, device_id_type=MESH,
            )

        started.append((cond, copy))
        when(cond, lambda: copy().start())

    def arrived(ref, sem, cond=None):
        def wait():
            pltpu.make_async_remote_copy(
                src_ref=ref, dst_ref=ref, send_sem=send_sem.at[0], recv_sem=sem,
                device_id=neighbours[0], device_id_type=MESH,
            ).wait_recv()

        when(cond, wait)

    class Plane:
        def __init__(self, buf, sem, parts):
            self.buf, self.sem, self.parts = buf, sem, parts

        def at(self, dx, dh, part):
            slot = lax.rem(x + dx, 4) * 4 + lax.rem(h + dh, 4)
            lo, n = self.parts[part]
            return self.buf.at[slot, pl.ds(lo, n)]

        def wait(self, dx, dh, part):
            arrived(self.at(dx, dh, part), self.sem.at[(dx * 4 + dh) * len(self.parts) + part])

        def send(self, dx, dh, part, ax, step):
            to_dx = (dx - step) % 4 if ax == "x" else dx
            to_dh = (dh - step) % 4 if ax == "h" else dh
            target = dev(dx=step) if ax == "x" else dev(dh=step)
            sem = self.sem.at[(to_dx * 4 + to_dh) * len(self.parts) + part]
            push(self.at(dx, dh, part), sem, target)

        def both(self, dx, dh, part, ax):
            for step in (1, -1):
                self.send(dx, dh, part, ax, step)

        def own(self, part):
            self.both(0, 0, part, "h")
            self.both(0, 0, part, "x")

        def near_h(self, dh, part):
            step = 1 if dh == 3 else -1
            self.wait(0, dh, part)
            if (part in PLUS_PARTS[0]) == (step == 1):
                self.send(0, dh, part, "h", step)
            self.both(0, dh, part, "x")

        def far_h(self, part):
            self.wait(0, 2, part)
            self.both(0, 2, part, "x")

        def near_x(self, dh, part):
            for dx in (3, 1):
                step = 1 if dx == 3 else -1
                self.wait(dx, dh, part)
                if (part in PLUS_PARTS[dh]) == (step == 1):
                    self.send(dx, dh, part, "x", step)

    THREE = (0, 1, 2)
    row_plane = Plane(rows, row_sem, ((0, 1), (1, 1), (2, 1)))

    half = NZ // 2
    FAR = {1: (0, 1), -1: (1, 2)}

    class Strip:
        def __init__(self, buf, hi, lo, z_sem, y_sem, sib_sem, held):
            self.buf, self.hi, self.lo, self.held = buf, hi, lo, held
            self.z_sem, self.y_sem, self.sib_sem = z_sem, y_sem, sib_sem

        def index(self, dz, flip_l, flip_o):
            zz = lax.rem(z + dz + NZ, NZ)
            ll = 1 - l if flip_l else l
            oo = 1 - o if flip_o else o
            return (zz * 2 + ll) * 2 + oo

        def tile(self, dz, flip_l, flip_o, lo=0, n=RB):
            return self.buf.at[pl.ds(self.index(dz, flip_l, flip_o) * RB + lo, n)]

        def cond(self, dz, flip_l, flip_o):
            return self.held(self.index(dz, flip_l, flip_o)) if self.held else None

        def z_at(self, dz, part=0, flip=False):
            k = (dz + half) if part == 0 else 2 * half + 1
            return self.z_sem.at[k + (2 * half + 2 if flip else 0)]

        def sib_at(self, dz, flip):
            return self.sib_sem.at[(dz + half) * 2 + int(flip)]

        def unpack(self, dz, flip_l, flip_o):
            def body():
                first = self.index(dz, flip_l, flip_o) * RB
                for b in range(RB):
                    t = self.buf[first + b]
                    s = turn(t)
                    for part, v in enumerate((jnp.where(left, t, s), jnp.where(left, s, t))):
                        hi, lo = split(v)
                        self.hi[first + b, 2 * part : 2 * part + 2] = hi.reshape(2, 16, 128)
                        self.lo[first + b, 2 * part : 2 * part + 2] = lo.reshape(2, 16, 128)

            when(self.cond(dz, flip_l, flip_o), body)

        def start_z(self, flip=False):
            cond, t = self.cond(0, flip, False), self.tile(0, flip, False)
            for k in (1, 3, 2):
                for step in (1, -1):
                    push(t, self.z_at(-k * step, 0, flip), dev(dz=k * step), cond=cond)

        def to_sibling(self, dz, flip):
            cond, t = self.cond(dz, flip, False), self.tile(dz, flip, False)
            push(t, self.sib_at(dz, flip), dev(flip_o=True), cond=cond)

        def across(self, dz):
            t = self.tile(dz, False, False)
            push(t, self.y_sem.at[dz + half], dev(flip_l=True))
            self.to_sibling(dz, False)

        def from_z(self, dz, flip=False):
            cond, t = self.cond(dz, flip, False), self.tile(dz, flip, False)
            arrived(t, self.z_at(dz, 0, flip), cond)
            step = 1 if dz < 0 else -1
            for k in ONWARD.get(abs(dz), ()):
                if abs(dz) + k == half:
                    part = self.tile(dz, flip, False, *FAR[step])
                    push(part, self.z_at(half, int(step < 0), flip), dev(dz=k * step), cond=cond)
                else:
                    push(t, self.z_at(dz - k * step, 0, flip), dev(dz=k * step), cond=cond)

        def near_z(self, dz):
            self.from_z(dz)
            self.across(dz)

        def both_from_z(self, dz):
            for flip in (False, True):
                self.from_z(dz, flip)
            for flip in (False, True):
                self.to_sibling(dz, flip)

        def opposite_from_z(self, flip=False):
            for step in (1, -1):
                part = self.tile(half, flip, False, *FAR[step])
                arrived(part, self.z_at(half, int(step < 0), flip), self.cond(half, flip, False))

        def other_plane(self, dz):
            cond, t = self.cond(dz, True, False), self.tile(dz, True, False)
            arrived(t, self.y_sem.at[dz + half], cond)
            push(t, self.sib_at(dz, True), dev(flip_o=True), cond=cond)
            self.unpack(dz, True, False)

        def from_sibling(self, dz, flip):
            arrived(self.tile(dz, flip, True), self.sib_at(dz, flip), self.cond(dz, flip, True))
            self.unpack(dz, flip, True)

    NEAR = (1, -1, 3, -3, 2, -2)
    FARTHER = (4, -4, 5, -5)
    main = Strip(strip, dup_hi, dup_lo, z_sem, y_sem, sib_sem, None)

    g = h // 2
    twin = (r, x * 4 + 3 - h)
    twin_c = x * 4 + 3 - h

    def held(index):
        return lax.rem(index // 6, 2) == g

    mine = held(r)
    other = Strip(twin_strip, twin_hi, twin_lo, twin_z_sem, None, twin_sib_sem, held)

    main.start_z()
    main.across(0)
    for part in THREE:
        row_plane.own(part)
    own_tile = main.tile(0, False, False)
    for k, target in enumerate((twin, neighbours[-1])):
        there = other.tile(0, False, False)
        push(own_tile, twin_sem.at[k], target, dst=there, cond=jnp.logical_not(mine))
    loads[3].wait()
    main.unpack(0, False, False)
    main.other_plane(0)
    main.from_sibling(0, False)
    for dh in (3, 1):
        for part in THREE:
            row_plane.near_h(dh, part)
    for dz in NEAR:
        main.near_z(dz)
    for part in THREE:
        row_plane.near_x(0, part)
    for dz in NEAR:
        main.unpack(dz, False, False)
    for part in THREE:
        row_plane.far_h(part)
    main.from_sibling(0, True)
    for dz in NEAR:
        main.from_sibling(dz, False)
    for dh in (3, 1):
        for part in THREE:
            row_plane.near_x(dh, part)
    for dz in (1, -1, 3, -3):
        main.other_plane(dz)
    for dz in FARTHER:
        main.near_z(dz)
    main.opposite_from_z()
    main.across(half)
    for k in (0, 1):
        flip = k == 1
        arrived(other.tile(0, flip, False), twin_sem.at[k], other.cond(0, flip, False))
        other.start_z(flip)
    for part in THREE:
        row_plane.near_x(2, part)
    for flip in (False, True):
        other.to_sibling(0, flip)
    for dz in (2, -2):
        main.other_plane(dz)
    for dz in FARTHER + (6,):
        main.unpack(dz, False, False)
    for dz in NEAR:
        main.from_sibling(dz, True)
    for dh in range(4):
        for part in THREE:
            row_plane.wait(2, dh, part)
    for dz in FARTHER + (6,):
        main.from_sibling(dz, False)
    for dz in FARTHER + (6,):
        main.other_plane(dz)
    for dz in FARTHER + (6,):
        main.from_sibling(dz, True)

    q_of = lax.broadcasted_iota(jnp.int32, (16, 256), 1) // 64

    def targets(col, row):
        v = jnp.zeros((16, 256), jnp.int32)
        for q in range(QS):
            v = jnp.where(q_of == q, pct_ref[col, q, row], v)
        return v

    def right(inner, target, col, hi_ref, lo_ref):
        his, los = [], []
        for k in inner:
            m = jnp.where(target == bct_ref[col, k], 1.0, 0.0).astype(BF16)
            for ref, got in ((hi_ref, his), (lo_ref, los)):
                v = ref[k]
                v = jnp.concatenate([v, v], axis=2) * m[None]
                got.append(v.reshape(64, 256))
        return jnp.concatenate(his, axis=0), jnp.concatenate(los, axis=0)

    def product(lhs, inner, target, col=c, hi_ref=dup_hi, lo_ref=dup_lo):
        r_hi, r_lo = right(inner, target, col, hi_ref, lo_ref)
        l_hi, l_lo = split(lhs)
        both = jnp.dot(jnp.concatenate([l_hi, l_lo], axis=0), r_hi, preferred_element_type=F32)
        return both[:64] + both[64:] + jnp.dot(l_hi, r_lo, preferred_element_type=F32)

    wanted = [targets(c, r * RB + i) for i in range(RB)]
    twin_wanted = [targets(twin_c, r * RB + i) for i in range(RB)]

    def square(i):
        acc = jnp.zeros((64, 256), F32)
        for g in range(4):
            t = [rows[g * 4 + s, i] for s in range(4)]
            s = [turn(v) for v in t]
            top = [jnp.where(left, t[0], s[1]), jnp.where(left, t[2], s[3])]
            low = [jnp.where(left, s[0], t[1]), jnp.where(left, s[2], t[3])]
            lhs = jnp.concatenate(
                [jnp.concatenate(top, axis=1), jnp.concatenate(low, axis=1)], axis=0
            )
            inner = [(g * 4 + s) * SEG + bct_ref[g * 4 + s, r * RB + i] for s in range(4)]
            acc = acc + product(lhs, inner, wanted[i])
        return acc

    mate_h = h + 1 - 2 * lax.rem(h, 2)
    mate = (r, x * 4 + mate_h)

    def slot(dx, e):
        return lax.rem(x + dx, 4) * 4 + (mate_h if e else h)

    PARTS = ((0, 64), (64, 64), (128, 32), (160, 32))
    PLUS = ((0, 3), (1, 2))

    def sq_at(dx, e, i):
        return squares.at[slot(dx, e), pl.ds(*PARTS[i])]

    def sq_sem_at(dx, e, i):
        return sq_sem.at[(dx * 2 + e) * 4 + i]

    def sq_wait(dx, e, i):
        arrived(sq_at(dx, e, i), sq_sem_at(dx, e, i))

    def sq_along_x(e, i):
        for step in (1, -1):
            push(sq_at(0, e, i), sq_sem_at(-step % 4, e, i), dev(dx=step))

    def sq_near_x(e, i):
        for dx in (3, 1):
            step = 1 if dx == 3 else -1
            sq_wait(dx, e, i)
            if (i in PLUS[e]) == (step == 1):
                push(sq_at(dx, e, i), sq_sem_at(2, e, i), dev(dx=step))

    def cubes(i, *tiles):
        row = r * RB + i
        for to, want, col, refs in (
            (twin_cube, twin_wanted, twin_c, (twin_hi, twin_lo)), (cube, wanted, c, (dup_hi, dup_lo))
        ):
            for dx, e in tiles:
                p = slot(dx, e)
                inner = [p * SEG + pct_ref[p, u, row] for u in range(QS)]
                v = product(squares[p, pl.ds(64 * i, 64)], inner, want[i], col, *refs)
                to[i] = v if (dx, e) == (0, 0) else to[i] + v
            if (2, 1) in tiles and to is twin_cube:
                push(to.at[i], back_sem.at[i], twin, dst=back_cube.at[i])

    for i in range(RB):
        squares[c, pl.ds(64 * i, 64)] = square(i)
        for part in (i,) if i < 2 else (2, 3):
            push(sq_at(0, 0, part), sq_sem_at(0, 1, part), mate)
            sq_along_x(0, part)
    for dz in (3, -3):
        other.both_from_z(dz)
    for part in range(4):
        sq_near_x(0, part)
        sq_wait(0, 1, part)
        sq_along_x(1, part)
    for dz in (2, -2, 1, -1) + FARTHER:
        other.both_from_z(dz)
    for flip in (False, True):
        other.opposite_from_z(flip)
        other.to_sibling(half, flip)
    for dz in (0,) + NEAR + FARTHER + (6,):
        for flip in (False, True):
            other.unpack(dz, flip, False)
    for part in range(4):
        sq_near_x(1, part)
    for dz in (0,) + NEAR + FARTHER + (6,):
        for flip in (False, True):
            other.from_sibling(dz, flip)
    for i in range(RB):
        cubes(i, (0, 0), (3, 0), (1, 0), (0, 1))
    for i in range(RB):
        for part in (i,) if i < 2 else (2, 3):
            sq_wait(2, 0, part)
            sq_wait(2, 1, part)
        cubes(i, (2, 0), (3, 1), (1, 1), (2, 1))
    for i in range(RB):
        arrived(back_cube.at[i], back_sem.at[i])

    for i in range(RB):
        wide2 = 3.0 * squares[c, pl.ds(64 * i, 64)] - 2.0 * (cube[i] + back_cube[i])
        for side in range(2):
            wide[:, :] = wide2[:, 128 * side : 128 * side + 128]
            even = wide[pl.ds(0, 32, stride=2), :]
            odd = wide[pl.ds(1, 32, stride=2), :]
            out_ref[i, :, 2 * side, :] = jnp.where(left, even, turn(odd))
            out_ref[i, :, 2 * side + 1, :] = jnp.where(left, turn(even), odd)

    for cond, copy in started:
        when(cond, lambda copy=copy: copy().wait_send())


def per_device(blocks, block_cols, product_cols, group_sizes):
    vmem = pl.BlockSpec(memory_space=pltpu.VMEM)
    out = pl.pallas_call(
        kernel,
        out_shape=jax.ShapeDtypeStruct((RB, 32, QS, 128), F32),
        in_specs=[pl.BlockSpec(memory_space=pl.ANY)] * 4,
        out_specs=vmem,
        scratch_shapes=[
            pltpu.VMEM((RB, 32, 128), F32),
            pltpu.SMEM((N_COL, NB), jnp.int32),
            pltpu.SMEM((N_COL, QS, NB), jnp.int32),
            pltpu.SMEM((NB,), jnp.int32),
            pltpu.SemaphoreType.DMA((4,)),
            pltpu.VMEM((NB, 32, 128), F32),
            pltpu.VMEM((N_COL, RB, 32, 128), F32),
            pltpu.VMEM((N_COL, RB * 64, 256), F32),
            pltpu.VMEM((NB, 4, 16, 128), BF16),
            pltpu.VMEM((NB, 4, 16, 128), BF16),
            pltpu.VMEM((RB, 64, 256), F32),
            pltpu.VMEM((64, 128), F32),
            pltpu.VMEM((NB, 32, 128), F32),
            pltpu.VMEM((NB, 4, 16, 128), BF16),
            pltpu.VMEM((NB, 4, 16, 128), BF16),
            pltpu.VMEM((RB, 64, 256), F32),
            pltpu.VMEM((RB, 64, 256), F32),
            pltpu.SemaphoreType.DMA((200,)),
            pltpu.SemaphoreType.DMA((28,)),
            pltpu.SemaphoreType.DMA((13,)),
            pltpu.SemaphoreType.DMA((26,)),
            pltpu.SemaphoreType.DMA((48,)),
            pltpu.SemaphoreType.DMA((32,)),
            pltpu.SemaphoreType.DMA((2,)),
            pltpu.SemaphoreType.DMA((28,)),
            pltpu.SemaphoreType.DMA((26,)),
            pltpu.SemaphoreType.DMA((3,)),
        ],
        compiler_params=pltpu.CompilerParams(
            collective_id=0, has_side_effects=True, vmem_limit_bytes=56 * 1024 * 1024
        ),
    )(
        blocks.reshape(RB, 32, 128),
        block_cols.T,
        jnp.transpose(product_cols, (1, 2, 0)),
        group_sizes,
    )
    return jnp.transpose(out, (0, 2, 1, 3)).reshape(RB, 1, QS, 4096)


def solution(mesh):
    return jax.shard_map(
        per_device,
        mesh=mesh,
        in_specs=(P("row", "col", None), P(), P(), P()),
        out_specs=P("row", "col", None, None),
        check_vma=False,
    )
```
